32 devices in a mesh: gx: 8 (over y, x, core), gy: 4 (over z).
Axes of the slice: x: 2, y: 2, z: 4, core: 2. Of those that a mesh axis runs over, the one named last changes fastest.
Arguments:
- tokens: bfloat16 [2, 16, 32, 32, 512], P(None, None, 'gx', 'gy'), may hold values from -6 to 6
- norm_gain: float32 [512], replicated, may hold values from 0.1 to 1.9
- w_qkv: bfloat16 [512, 1536], replicated, may hold values from -12 to 12
- w_out: bfloat16 [512, 512], replicated, may hold values from -1 to 1
Outputs:
- result: bfloat16 [2, 16, 32, 32, 512], P(None, None, 'gx', 'gy')
The draws below stay inside these ranges and needn't reach their ends.
All inputs are finite; a program needn't handle non-finite values.
Results may differ from the reference program's by a relative error of at most 0.0095.
Values may be sent and summed in bfloat16 or wider, within the bound.
No kernel may reach another device: no remote copies, remote signals or barrier semaphores. Data moves between devices by JAX's collectives and lax.ppermute only.
A program may use at most 64 MiB of HBM per device.

```python
import jax
import jax.numpy as jnp
from jax import lax

D = 512
HEADS = 8
TSTEPS = 16
BATCH = 2
NX = 32
NY = 32


def draw_w_qkv(key, part):
    primary = jnp.clip(jax.random.normal(jax.random.fold_in(key, 11), (D, 3 * D), jnp.float32), -4.0, 4.0) / jnp.sqrt(jnp.float32(D))
    return primary.astype(jnp.bfloat16)


def shard_levels(key, dims, pieces, least, high):
    factor_of, own = 1.0, jax.random.fold_in(key, 6)
    for axis_at, shards_of in pieces:
        steps = jnp.exp(jax.random.uniform(jax.random.fold_in(own, axis_at), (shards_of,), jnp.float32, least / len(pieces), high / len(pieces)))
        factor_of = factor_of * jnp.repeat(steps, dims[axis_at] // shards_of).reshape([-1 if axis == axis_at else 1 for axis in range(len(dims))])
    return factor_of


def scatter_about(own_key, extent, spread, reach, shards=(), kind=jnp.bfloat16):
    values = spread * jax.random.normal(own_key, extent, jnp.float32)
    if shards:
        values = values * shard_levels(own_key, extent, shards, -0.22, 0.18)
    return jnp.clip(values, -reach, reach).astype(kind)


def setup_inputs(seed: int = 0) -> dict:
    key_list = jax.random.split(jax.random.key(seed), 5)
    return {
        "tokens": scatter_about(key_list[0], (BATCH, TSTEPS, NX, NY, D), 1.0, 6.0, ((2, 8), (3, 4))),
        "norm_gain": jnp.clip(1.0 + 0.18 * jax.random.normal(key_list[1], (D,), jnp.float32), 0.1, 1.9),
        "w_qkv": draw_w_qkv(jax.random.fold_in(key_list[4], 71), 0),
        "w_out": scatter_about(key_list[3], (D, D), (D // 16) ** -0.5, 1.0),
    }


def attend(triple, seq_dim):
    shape = triple.shape
    width = shape[-1] // 3
    head_size = width // HEADS
    split = shape[:-1] + (HEADS, head_size)
    queries = triple[..., :width].reshape(split).astype(jnp.float32)
    key_part = triple[..., width:2 * width].reshape(split).astype(jnp.float32)
    values = triple[..., 2 * width:].reshape(split).astype(jnp.float32)
    if seq_dim == 1:
        form_scores, form_mix = ('asche,atche->achst', 'achst,atche->asche')
    else:
        form_scores, form_mix = ('acshe,acthe->achst', 'achst,acthe->acshe')
    scores = jnp.einsum(form_scores, queries, key_part) / jnp.sqrt(jnp.float32(head_size))
    highest = lax.optimization_barrier(jnp.max(scores, axis=-1, keepdims=True))
    expo = jnp.exp(scores - highest)
    weights = (expo / lax.optimization_barrier(jnp.sum(expo, axis=-1, keepdims=True))).astype(jnp.bfloat16)
    mixed = jnp.einsum(form_mix, weights.astype(jnp.float32), values)
    return mixed.reshape(shape[:-1] + (width,)).astype(jnp.bfloat16)

def reference(tokens, norm_gain, w_qkv, w_out):
    batch, steps, cells_x, cells_y, width = tokens.shape
    field = tokens.astype(jnp.float32)
    normed = (field * lax.rsqrt(lax.optimization_barrier(jnp.mean(field * field, axis=-1, keepdims=True)) + 1e-05) * norm_gain).astype(jnp.bfloat16)
    triple = jnp.dot(normed.reshape(-1, width), w_qkv, preferred_element_type=jnp.float32).astype(jnp.bfloat16)
    triple = triple.reshape(batch, steps, cells_x, cells_y, 3 * width)
    along_time = lax.map(lambda sample: attend(sample.reshape(1, steps, cells_x * cells_y, 3 * width), 1), triple)
    along_time = along_time.reshape(batch, steps, cells_x, cells_y, width)
    flat = triple.reshape(batch * steps, cells_x, cells_y, 3 * width)
    along_x = lax.map(lambda plane: attend(plane[None], 1)[0], flat)
    along_y = lax.map(lambda plane: attend(plane[None], 2)[0], flat)
    mixed = (along_time.astype(jnp.float32) + along_x.reshape(along_time.shape).astype(jnp.float32) + along_y.reshape(along_time.shape).astype(jnp.float32)).astype(jnp.bfloat16)
    update = jnp.dot(mixed.reshape(-1, width), w_out, preferred_element_type=jnp.float32)
    return (field + update.reshape(field.shape)).astype(jnp.bfloat16)
```

```python
import functools
import math

import jax
import jax.numpy as jnp
from jax import lax
from jax.experimental import pallas as pl
from jax.experimental.pallas import tpu as pltpu
from jax.sharding import PartitionSpec as P

HEADS = 8
MASKED = -1e30
Y_CHUNKS = 2
VMEM = pl.BlockSpec(memory_space=pltpu.VMEM)
ANY = pl.BlockSpec(memory_space=pl.ANY)
PARAMS = pltpu.CompilerParams(vmem_limit_bytes=48 * 1024 * 1024)


def normalize(field, gain):
    scale = lax.rsqrt(jnp.mean(field * field, axis=-1, keepdims=True) + 1e-05)
    return (field * scale * gain).astype(jnp.bfloat16)


def line_bias(block, line_of):
    key_at = lax.broadcasted_iota(jnp.int32, (block, 2 * block), 0)
    query_at = lax.rem(lax.broadcasted_iota(jnp.int32, (block, 2 * block), 1), block)
    return jnp.where(line_of(key_at) == line_of(query_at), 0.0, MASKED).astype(jnp.float32)


def project(normed_ref, w_ref, w_values_ref, qk_ref, values_ref):
    total, width = normed_ref.shape
    step = min(256, total)
    for at in range(0, total, step):
        rows = normed_ref[at : at + step]
        qk_ref[at : at + step] = jnp.dot(
            rows, w_ref[:, : 2 * width], preferred_element_type=jnp.float32
        ).astype(jnp.bfloat16)
        values_ref[:, at : at + step] = lax.dot_general(
            w_values_ref[...], rows, (((1,), (1,)), ((), ())), preferred_element_type=jnp.float32
        ).astype(jnp.bfloat16)


def attend(qk, values, bias):
    block, width = qk.shape[0], qk.shape[1] // 2
    size = width // HEADS
    factor = math.log2(math.e) / math.sqrt(size)
    lane = lax.broadcasted_iota(jnp.int32, (block, 2 * size), 1)
    mixed = []
    for at in range(0, width, 2 * size):
        queries = qk[:, at : at + 2 * size]
        key_part = qk[:, width + at : width + at + 2 * size]
        zero = jnp.zeros_like(queries)
        pair = jnp.concatenate(
            [jnp.where(lane < size, queries, zero), jnp.where(lane < size, zero, queries)], axis=0
        )
        scores = lax.dot_general(
            key_part, pair, (((1,), (1,)), ((), ())), preferred_element_type=jnp.float32
        )
        scores = scores + bias
        expo = jnp.exp2((scores - jnp.max(scores, axis=0, keepdims=True)) * factor)
        inverse = 1.0 / jnp.sum(expo, axis=0, keepdims=True)
        expo = expo.astype(jnp.bfloat16)
        for head in range(2):
            rows = slice(at + head * size, at + (head + 1) * size)
            columns = slice(head * block, (head + 1) * block)
            summed = jnp.dot(values[rows], expo[:, columns], preferred_element_type=jnp.float32)
            mixed.append(summed * inverse[:, columns])
    return jnp.concatenate(mixed, axis=0)


def attention_scratch(total, block, width):
    return [
        pltpu.VMEM((total, width), jnp.bfloat16),
        pltpu.VMEM((total, 2 * width), jnp.bfloat16),
        pltpu.VMEM((width, total), jnp.bfloat16),
        pltpu.VMEM((block, 2 * block), jnp.float32),
    ]


def time_kernel(
    gain_ref, w_ref, w_values_ref, tokens_ref, out_ref, normed_ref, qk_ref, values_ref, bias_ref
):
    batch, steps, cells_x, cells_y, width = tokens_ref.shape
    block = steps * cells_y
    bias_ref[...] = line_bias(block, lambda at: lax.rem(at, cells_y))
    places = [(b, x) for b in range(batch) for x in range(cells_x)]
    for index, (b, x) in enumerate(places):
        field = tokens_ref[b, :, x].astype(jnp.float32).reshape(block, width)
        normed_ref[index * block : (index + 1) * block] = normalize(field, gain_ref[...])
    project(normed_ref, w_ref, w_values_ref, qk_ref, values_ref)
    for index, (b, x) in enumerate(places):
        rows = slice(index * block, (index + 1) * block)
        out = attend(qk_ref[rows], values_ref[:, rows], bias_ref[...]).T
        out_ref[b, :, x] = out.reshape(steps, cells_y, width).astype(jnp.bfloat16)


def attend_time(tokens, gain, w_qkv, w_values):
    batch, steps, cells_x, cells_y, width = tokens.shape
    block = steps * cells_y
    return pl.pallas_call(
        time_kernel,
        out_shape=jax.ShapeDtypeStruct(tokens.shape, tokens.dtype),
        in_specs=[VMEM] * 4,
        out_specs=VMEM,
        scratch_shapes=attention_scratch(batch * cells_x * block, block, width),
        compiler_params=PARAMS,
        name="attend_time",
    )(gain, w_qkv, w_values, tokens)


def planes_attention(parts, outs, line_of, gain_ref, w_ref, w_values_ref, scratch):
    normed_ref, qk_ref, values_ref, bias_ref = scratch
    block = bias_ref.shape[0]
    planes = normed_ref.shape[0] // block
    bias_ref[...] = line_bias(block, line_of)
    for plane in range(planes):
        field = jnp.concatenate([part(plane) for part in parts], axis=0)
        normed_ref[plane * block : (plane + 1) * block] = normalize(field, gain_ref[...])
    project(normed_ref, w_ref, w_values_ref, qk_ref, values_ref)
    for plane in range(planes):
        rows = slice(plane * block, (plane + 1) * block)
        out = attend(qk_ref[rows], values_ref[:, rows], bias_ref[...]).T
        each = block // len(parts)
        for index, put in enumerate(outs):
            put(plane, out[index * each : (index + 1) * each])


def y_kernel(count, gain_ref, w_ref, w_values_ref, *refs):
    pieces, results, scratch = refs[:count], refs[count : 2 * count], refs[2 * count :]
    _, cells_x, cells_y, width = pieces[0].shape

    def part(ref):
        return lambda plane: ref[plane].astype(jnp.float32).reshape(cells_x * cells_y, width)

    def put(ref):
        def store(plane, value):
            ref[plane] = value.reshape(cells_x, cells_y, width).astype(jnp.bfloat16)

        return store

    planes_attention(
        [part(ref) for ref in pieces],
        [put(ref) for ref in results],
        lambda at: lax.rem(lax.div(at, cells_y), cells_x),
        gain_ref,
        w_ref,
        w_values_ref,
        scratch,
    )


def attend_y(pieces, gain, w_qkv, w_values):
    count = len(pieces)
    planes, cells_x, cells_y, width = pieces[0].shape
    block = count * cells_x * cells_y
    return pl.pallas_call(
        functools.partial(y_kernel, count),
        out_shape=[jax.ShapeDtypeStruct(piece.shape, piece.dtype) for piece in pieces],
        in_specs=[VMEM] * (3 + count),
        out_specs=[VMEM] * count,
        scratch_shapes=attention_scratch(planes * block, block, width),
        compiler_params=PARAMS,
        name="attend_y",
    )(gain, w_qkv, w_values, *pieces)


def x_kernel(count, gain_ref, w_ref, w_values_ref, *refs):
    pieces, sibling = refs[:count], refs[count]
    results, scratch = refs[count + 1 : 2 * count + 1], refs[2 * count + 1 :]
    _, _, cells_x, cells_y, width = pieces[0].shape
    core = lax.rem(lax.axis_index("gx"), 2)

    def part(ref, index):
        return lambda plane: ref[index, plane].astype(jnp.float32).reshape(cells_x * cells_y, width)

    def put(ref, index):
        def store(plane, value):
            ref[index, plane] = value.reshape(cells_x, cells_y, width).astype(jnp.bfloat16)

        return store

    planes_attention(
        [part(ref, core) for ref in pieces] + [part(sibling, at) for at in range(count)],
        [put(ref, 0) for ref in results] + [put(ref, 1) for ref in results],
        lambda at: lax.rem(at, cells_y),
        gain_ref,
        w_ref,
        w_values_ref,
        scratch,
    )


def attend_x(pieces, sibling, gain, w_qkv, w_values):
    count = len(pieces)
    _, planes, cells_x, cells_y, width = pieces[0].shape
    block = 2 * count * cells_x * cells_y
    return pl.pallas_call(
        functools.partial(x_kernel, count),
        out_shape=[jax.ShapeDtypeStruct(piece.shape, piece.dtype) for piece in pieces],
        in_specs=[VMEM] * (4 + count),
        out_specs=[VMEM] * count,
        scratch_shapes=attention_scratch(planes * block, block, width),
        compiler_params=PARAMS,
        name="attend_x",
    )(gain, w_qkv, w_values, *pieces, sibling)


def base_kernel(count, along_time_ref, *refs):
    pieces, sibling, out_ref = refs[:count], refs[count], refs[count + 1]
    planes = pieces[0].shape[1]
    device = lax.axis_index("gx")
    chip, core = device // 2, lax.rem(device, 2)
    for index in range(count):
        for lane, source in ((core, pieces[index].at[0]), (1 - core, sibling.at[index])):
            at = pl.ds(((chip ^ index) * 2 + lane) * planes, planes)
            out_ref[at] = along_time_ref[at].astype(jnp.float32) + source[...].astype(jnp.float32)


def add_x(along_time, pieces, sibling):
    return pl.pallas_call(
        functools.partial(base_kernel, len(pieces)),
        out_shape=jax.ShapeDtypeStruct(along_time.shape, jnp.float32),
        in_specs=[VMEM] * (2 + len(pieces)),
        out_specs=VMEM,
        compiler_params=PARAMS,
        name="add_x",
    )(along_time, *pieces, sibling)


def final_kernel(count, chunk, w_ref, tokens_ref, base_ref, *refs):
    pieces = refs[:count]
    out_ref, held, sems = refs[-3:]
    planes, cells_x, cells_y, width = pieces[0].shape
    group = tokens_ref.shape[0] // count
    me = lax.axis_index("gy")
    copies = []
    for index in range(count):
        at = pl.ds((me ^ index) * group + chunk * planes, planes)
        mixed = base_ref[at] + pieces[index][...].astype(jnp.float32)
        mixed = mixed.reshape(planes * cells_x * cells_y, width).astype(jnp.bfloat16)
        update = jnp.dot(mixed, w_ref[...], preferred_element_type=jnp.float32)
        field = tokens_ref[at].astype(jnp.float32)
        held[index] = (field + update.reshape(field.shape)).astype(jnp.bfloat16)
        copies.append(pltpu.make_async_copy(held.at[index], out_ref.at[at], sems.at[index]))
        copies[-1].start()
    for copy in copies:
        copy.wait()


def finish(chunk, w_out, tokens, base, pieces, result):
    count = len(pieces)
    earlier = [] if result is None else [result]
    return pl.pallas_call(
        functools.partial(final_kernel, count, chunk),
        out_shape=jax.ShapeDtypeStruct(tokens.shape, tokens.dtype),
        in_specs=[VMEM] * (3 + count) + [ANY] * len(earlier),
        out_specs=ANY,
        scratch_shapes=[
            pltpu.VMEM((count,) + pieces[0].shape, tokens.dtype),
            pltpu.SemaphoreType.DMA((count,)),
        ],
        input_output_aliases={3 + count: 0} if earlier else {},
        compiler_params=PARAMS,
        name="finish",
    )(w_out, tokens, base, *pieces, *earlier)


def exchange(value, axis, size, flip):
    return lax.ppermute(value, axis, [(at, at ^ flip) for at in range(size)])


def body(count_x, count_y, tokens, norm_gain, w_qkv, w_out):
    batch, steps, cells_x, cells_y, width = tokens.shape
    lines = batch * steps
    plane_shape = (cells_x, cells_y, width)
    gain = norm_gain.reshape(1, width)
    chips = count_x // 2
    device_x, device_y = lax.axis_index("gx"), lax.axis_index("gy")
    chip, core = device_x // 2, lax.rem(device_x, 2)
    chunks = math.gcd(Y_CHUNKS, lines // count_y)
    chunk_planes = lines // count_y // chunks

    by_y = tokens.reshape((count_y, chunks, chunk_planes) + plane_shape)
    y_pieces = []
    for chunk in range(chunks):
        pieces = [by_y[device_y ^ flip, chunk] for flip in range(count_y)]
        y_pieces.append(
            [p if flip == 0 else exchange(p, "gy", count_y, flip) for flip, p in enumerate(pieces)]
        )
    by_x = tokens.reshape((chips, 2, lines // count_x) + plane_shape)
    x_pieces = [by_x[chip ^ flip] for flip in range(chips)]
    x_pieces = [
        p if flip == 0 else exchange(p, "gx", count_x, 2 * flip) for flip, p in enumerate(x_pieces)
    ]
    sibling = exchange(jnp.stack([p[1 - core] for p in x_pieces]), "gx", count_x, 1)

    w_values = w_qkv[:, 2 * width :].T
    along_time = attend_time(tokens, gain, w_qkv, w_values).reshape((lines,) + plane_shape)

    x_pieces = attend_x(x_pieces, sibling, gain, w_qkv, w_values)
    x_pieces = [
        p if flip == 0 else exchange(p, "gx", count_x, 2 * flip) for flip, p in enumerate(x_pieces)
    ]
    sibling = exchange(jnp.stack([p[1] for p in x_pieces]), "gx", count_x, 1)
    base = add_x(along_time, x_pieces, sibling)

    result = None
    flat = tokens.reshape((lines,) + plane_shape)
    returned = []
    for pieces in y_pieces:
        pieces = attend_y(pieces, gain, w_qkv, w_values)
        returned.append(
            [p if flip == 0 else exchange(p, "gy", count_y, flip) for flip, p in enumerate(pieces)]
        )
    for chunk, pieces in enumerate(returned):
        result = finish(chunk, w_out, flat, base, pieces, result)
    return result.reshape(tokens.shape)


def solution(mesh):
    placed = (P(None, None, "gx", "gy", None), P(), P(), P())
    return jax.shard_map(
        functools.partial(body, mesh.shape["gx"], mesh.shape["gy"]),
        mesh=mesh,
        in_specs=placed,
        out_specs=P(None, None, "gx", "gy", None),
        check_vma=False,
    )
```

```python
import functools
import math

import jax
import jax.numpy as jnp
from jax import lax
from jax.experimental import pallas as pl
from jax.experimental.pallas import tpu as pltpu
from jax.sharding import PartitionSpec as P

HEADS = 8
MASKED = -1e30
Y_CHUNKS = 2
BLOCK = 128
LANES = 128
KERNEL_US = 5


def cost(us):
    return pl.CostEstimate(
        flops=int(1000 + us * 1.15e9),
        bytes_accessed=int(1000 + us * 3.69e6),
        transcendentals=int(us * 1e6),
    )
ANY = pl.BlockSpec(memory_space=pl.ANY)
HBM = pl.BlockSpec(memory_space=pltpu.HBM)
VMEM = pl.BlockSpec(memory_space=pltpu.VMEM)


def params(block=0):
    return pltpu.CompilerParams(vmem_limit_bytes=max(24 * 1024 * 1024, 48 * block * block))


def start_copies(pairs, sems):
    copies = [
        pltpu.make_async_copy(source, target, sems.at[at])
        for at, (source, target) in enumerate(pairs)
    ]
    for copy in copies:
        copy.start()
    return copies


def normalize(field, gain):
    scale = lax.rsqrt(jnp.mean(field * field, axis=-1, keepdims=True) + 1e-05)
    return field * scale * gain


def line_bias(block, line_of):
    key_at = lax.broadcasted_iota(jnp.int32, (block, 2 * block), 0)
    query_at = lax.rem(lax.broadcasted_iota(jnp.int32, (block, 2 * block), 1), block)
    return jnp.where(line_of(key_at) == line_of(query_at), 0.0, MASKED).astype(jnp.float32)


def project(normed_ref, w_ref, w_values_ref, qk_ref, values_ref):
    total, width = normed_ref.shape
    step = min(256, total)
    for at in range(0, total, step):
        rows = normed_ref[at : at + step]
        qk_ref[at : at + step] = jnp.dot(
            rows, w_ref[:, : 2 * width], preferred_element_type=jnp.float32
        ).astype(jnp.bfloat16)
        values_ref[:, at : at + step] = lax.dot_general(
            w_values_ref[...], rows, (((1,), (1,)), ((), ())), preferred_element_type=jnp.float32
        ).astype(jnp.bfloat16)


def attend(qk, values, bias):
    block, width = qk.shape[0], qk.shape[1] // 2
    size = width // HEADS
    factor = math.log2(math.e) / math.sqrt(size)
    lane = lax.broadcasted_iota(jnp.int32, (block, 2 * size), 1)
    mixed = []
    for at in range(0, width, 2 * size):
        queries = qk[:, at : at + 2 * size]
        key_part = qk[:, width + at : width + at + 2 * size]
        zero = jnp.zeros_like(queries)
        pair = jnp.concatenate(
            [jnp.where(lane < size, queries, zero), jnp.where(lane < size, zero, queries)], axis=0
        )
        scores = lax.dot_general(
            key_part, pair, (((1,), (1,)), ((), ())), preferred_element_type=jnp.float32
        )
        scores = scores + bias
        expo = jnp.exp2((scores - jnp.max(scores, axis=0, keepdims=True)) * factor)
        inverse = 1.0 / jnp.sum(expo, axis=0, keepdims=True)
        expo = expo.astype(jnp.bfloat16)
        for head in range(2):
            rows = slice(at + head * size, at + (head + 1) * size)
            columns = slice(head * block, (head + 1) * block)
            summed = jnp.dot(values[rows], expo[:, columns], preferred_element_type=jnp.float32)
            mixed.append(summed * inverse[:, columns])
    return jnp.concatenate(mixed, axis=0).T


def attention_kernel(plan, gain_ref, w_ref, w_values_ref, *refs):
    operands, results = refs[: plan["operands"]], refs[plan["first_result"] : plan["scratch"]]
    normed_ref, qk_ref, values_ref, bias_ref, *order_refs = refs[plan["scratch"] :]
    block, count = plan["block"], plan["count"]
    bias_ref[...] = line_bias(block, plan["line_of"])
    for index in range(count):
        plan["norm"](index, operands, gain_ref[...], normed_ref, *order_refs)
    project(normed_ref, w_ref, w_values_ref, qk_ref, values_ref)
    each = normed_ref.shape[0] // count
    for index in range(count):
        for at in range(index * each, (index + 1) * each, block):
            out = attend(qk_ref[at : at + block], values_ref[:, at : at + block], bias_ref[...])
            plan["put"](index, at - index * each, out, results, *order_refs)


def attention(plan, total, out_shapes, operands, gain, w_qkv, w_values, after, name):
    width = w_qkv.shape[0]
    block = plan["block"]
    inputs = [gain, w_qkv, w_values, *operands, *after]
    plan = dict(
        plan,
        operands=len(operands),
        first_result=len(operands) + len(after),
        scratch=len(operands) + len(after) + len(out_shapes),
    )
    bf16, f32 = jnp.bfloat16, jnp.float32
    return pl.pallas_call(
        functools.partial(attention_kernel, plan),
        out_shape=[jax.ShapeDtypeStruct(shape, bf16) for shape in out_shapes],
        in_specs=[VMEM] * (3 + len(operands)) + [ANY] * len(after),
        out_specs=[VMEM] * len(out_shapes),
        scratch_shapes=[
            pltpu.VMEM((total, width), bf16),
            pltpu.VMEM((total, 2 * width), bf16),
            pltpu.VMEM((width, total), bf16),
            pltpu.VMEM((block, 2 * block), f32),
            *[pltpu.VMEM(shape, f32) for shape in plan["order"]],
        ],
        compiler_params=params(block),
        cost_estimate=cost(KERNEL_US),
        name=name,
    )(*inputs)


def attend_time(tokens, gain, w_qkv, w_values, after=()):
    batch, steps, cells_x, cells_y, width = tokens.shape
    block = steps * cells_y
    count = batch * cells_x

    def norm(index, operands, gain, normed):
        field = operands[0][index // cells_x, :, index % cells_x].astype(jnp.float32)
        field = normalize(field.reshape(block, width), gain)
        normed[index * block : (index + 1) * block] = field.astype(jnp.bfloat16)

    def put(index, at, out, results):
        field = out.reshape(steps, cells_y, width).astype(jnp.bfloat16)
        results[0][index // cells_x, :, index % cells_x] = field

    plan = dict(
        block=block,
        count=count,
        line_of=lambda at: lax.rem(at, cells_y),
        norm=norm,
        put=put,
        order=[],
    )
    return attention(
        plan, count * block, [tokens.shape], [tokens], gain, w_qkv, w_values, after, "attend_time"
    )[0]


def attend_y(pieces, first, planes, gain, w_qkv, w_values, after=()):
    size = len(pieces)
    _, cells_x, cells_y, width = pieces[0].shape
    block = size * cells_x * cells_y

    def norm(index, operands, gain, normed):
        field = jnp.concatenate(
            [ref[first + index].astype(jnp.float32).reshape(cells_x * cells_y, width) for ref in operands],
            axis=0,
        )
        normed[index * block : (index + 1) * block] = normalize(field, gain).astype(jnp.bfloat16)

    def put(index, at, out, results):
        field = out.reshape(size, cells_x, cells_y, width).astype(jnp.bfloat16)
        for part in range(size):
            results[part][index] = field[part]

    plan = dict(
        block=block,
        count=planes,
        line_of=lambda at: lax.rem(lax.div(at, cells_y), cells_x),
        norm=norm,
        put=put,
        order=[],
    )
    shapes = [(planes, cells_x, cells_y, width)] * size
    return attention(
        plan, planes * block, shapes, pieces, gain, w_qkv, w_values, after, "attend_y"
    )


def attend_x(pieces, gain, w_qkv, w_values, after=()):
    size, planes, cells_x, cells_y, width = pieces.shape
    chips = size // 2
    length = size * cells_x
    each = length * cells_y
    together = max(1, min(cells_y, BLOCK // length))
    block = together * length
    columns = [slice(at, at + LANES) for at in range(0, width, LANES)]

    def norm(index, operands, gain, normed, order):
        field = operands[0][:, index].astype(jnp.float32).reshape(each, width)
        field = normalize(field, gain)
        for part, lanes in enumerate(columns):
            order[part] = field[:, lanes]
        for y in range(cells_y):
            at = index * each + y * length
            for part, lanes in enumerate(columns):
                line = order[part, pl.ds(y, length, stride=cells_y), :]
                normed[at : at + length, lanes] = line.astype(jnp.bfloat16)

    def put(index, at, out, results, order):
        for line in range(together):
            rows = slice(line * length, (line + 1) * length)
            for part, lanes in enumerate(columns):
                where = pl.ds(at // length + line, length, stride=cells_y)
                order[part, where, :] = out[rows, lanes]
        if at + block < each:
            return
        device = lax.axis_index("gx")
        chip, core = device // 2, lax.rem(device, 2)
        per = cells_x * cells_y
        for flip in range(chips):
            for which, lane in enumerate((core, 1 - core)):
                start = pl.multiple_of(((chip ^ flip) * 2 + lane) * per, per)
                for part, lanes in enumerate(columns):
                    field = order[part, pl.ds(start, per), :].reshape(cells_x, cells_y, LANES)
                    results[flip][which, index, :, :, lanes] = field.astype(jnp.bfloat16)

    plan = dict(
        block=block,
        count=planes,
        line_of=lambda at: lax.div(at, length),
        norm=norm,
        put=put,
        order=[(width // LANES, each, LANES)],
    )
    shapes = [(2, planes, cells_x, cells_y, width)] * chips
    return attention(
        plan, planes * each, shapes, [pieces], gain, w_qkv, w_values, after, "attend_x"
    )


def pack_kernel(count, *refs):
    out, sems = refs[-2:]
    for copy in start_copies([(refs[at].at[1], out.at[at]) for at in range(count)], sems):
        copy.wait()


def pack(pieces):
    count = len(pieces)
    return pl.pallas_call(
        functools.partial(pack_kernel, count),
        out_shape=jax.ShapeDtypeStruct((count,) + pieces[0].shape[1:], pieces[0].dtype),
        in_specs=[VMEM] * count,
        out_specs=VMEM,
        scratch_shapes=[pltpu.SemaphoreType.DMA((count,))],
        compiler_params=params(),
        cost_estimate=cost(0),
        name="pack_x",
    )(*pieces)


def base_kernel(count, along_time_ref, *refs):
    pieces, sibling, out_ref = refs[:count], refs[count], refs[-1]
    planes = pieces[0].shape[1]
    device = lax.axis_index("gx")
    chip, core = device // 2, lax.rem(device, 2)
    for index in range(count):
        for lane, source in ((core, pieces[index].at[0]), (1 - core, sibling.at[index])):
            at = pl.ds(((chip ^ index) * 2 + lane) * planes, planes)
            out_ref[at] = along_time_ref[at].astype(jnp.float32) + source[...].astype(jnp.float32)


def add_x(along_time, pieces, sibling):
    return pl.pallas_call(
        functools.partial(base_kernel, len(pieces)),
        out_shape=jax.ShapeDtypeStruct(along_time.shape, jnp.float32),
        in_specs=[VMEM] * (2 + len(pieces)),
        out_specs=VMEM,
        compiler_params=params(),
        cost_estimate=cost(0),
        name="add_x",
    )(along_time, *pieces, sibling)


def final_kernel(size, chunk, w_ref, tokens_ref, base_ref, *refs):
    pieces = refs[:size]
    out_ref, held_ref, sems = refs[-3:]
    _, planes, cells_x, cells_y, width = held_ref.shape
    group = tokens_ref.shape[0] // size
    me = lax.axis_index("gy")
    storing = []
    for flip in range(size):
        where = pl.ds((me ^ flip) * group + chunk * planes, planes)
        mixed = base_ref[where] + pieces[flip][...].astype(jnp.float32)
        mixed = mixed.reshape(planes * cells_x * cells_y, width).astype(jnp.bfloat16)
        update = jnp.dot(mixed, w_ref[...], preferred_element_type=jnp.float32)
        field = tokens_ref[where].astype(jnp.float32)
        held_ref[flip] = (field + update.reshape(field.shape)).astype(jnp.bfloat16)
        copy = pltpu.make_async_copy(held_ref.at[flip], out_ref.at[where], sems.at[flip])
        copy.start()
        storing.append(copy)
    for copy in storing:
        copy.wait()


def finish(chunk, w_out, tokens, base, pieces, result):
    size = len(pieces)
    earlier = [] if result is None else [result]
    return pl.pallas_call(
        functools.partial(final_kernel, size, chunk),
        out_shape=jax.ShapeDtypeStruct(tokens.shape, tokens.dtype),
        in_specs=[VMEM] * (3 + size) + [ANY] * len(earlier),
        out_specs=ANY,
        scratch_shapes=[
            pltpu.VMEM((size,) + pieces[0].shape, tokens.dtype),
            pltpu.SemaphoreType.DMA((size,)),
        ],
        input_output_aliases={3 + size: 0} if earlier else {},
        compiler_params=params(),
        cost_estimate=cost(0),
        name="finish",
    )(w_out, tokens, base, *pieces, *earlier)


def cut_kernel(size, planes, tokens_ref, *refs):
    outs, sems = refs[:size], refs[-1]
    me = lax.axis_index("gy")
    pairs = [(tokens_ref.at[pl.ds((me ^ flip) * planes, planes)], outs[flip]) for flip in range(size)]
    for copy in start_copies(pairs, sems):
        copy.wait()


def cut(tokens, size, planes):
    piece = jax.ShapeDtypeStruct((planes,) + tokens.shape[1:], tokens.dtype)
    return pl.pallas_call(
        functools.partial(cut_kernel, size, planes),
        out_shape=[piece] * size,
        in_specs=[ANY],
        out_specs=[HBM] * size,
        scratch_shapes=[pltpu.SemaphoreType.DMA((size,))],
        compiler_params=params(),
        cost_estimate=cost(0),
        name="cut",
    )(tokens)


def trade(pieces, axis="gy", factor=1):
    size = factor * len(pieces)
    return [
        piece
        if flip == 0
        else lax.ppermute(piece, axis, [(at, at ^ (factor * flip)) for at in range(size)])
        for flip, piece in enumerate(pieces)
    ]


def body(count_x, count_y, tokens, norm_gain, w_qkv, w_out):
    batch, steps, cells_x, cells_y, width = tokens.shape
    lines = batch * steps
    plane_shape = (cells_x, cells_y, width)
    gain = norm_gain.reshape(1, width)
    chunks = math.gcd(Y_CHUNKS, lines // count_y)
    chunk_planes = lines // count_y // chunks
    flat = tokens.reshape((lines,) + plane_shape)
    w_values = w_qkv[:, 2 * width :].T

    swap = [(at, at ^ 1) for at in range(count_x)]
    y_pieces = trade(cut(flat, count_y, lines // count_y))
    along_time = attend_time(tokens, gain, w_qkv, w_values)
    x_pieces = lax.all_to_all(
        flat.reshape((count_x, lines // count_x) + plane_shape), "gx", 0, 0, tiled=True
    )
    along_x = attend_x(x_pieces, gain, w_qkv, w_values, [along_time])
    last = along_x[0]
    returned = []
    for chunk in range(chunks):
        out = attend_y(
            y_pieces, chunk * chunk_planes, chunk_planes, gain, w_qkv, w_values, [last]
        )
        last = out[0]
        returned.append(trade(out))
    along_x = trade(along_x, "gx", 2)
    sibling = lax.ppermute(pack(along_x), "gx", swap)
    base = add_x(along_time.reshape((lines,) + plane_shape), along_x, sibling)

    result = None
    for chunk, pieces in enumerate(returned):
        result = finish(chunk, w_out, flat, base, pieces, result)
    return result.reshape(tokens.shape)


def solution(mesh):
    placed = (P(None, None, "gx", "gy", None), P(), P(), P())
    return jax.shard_map(
        functools.partial(body, mesh.shape["gx"], mesh.shape["gy"]),
        mesh=mesh,
        in_specs=placed,
        out_specs=P(None, None, "gx", "gy", None),
        check_vma=False,
    )
```

```python
import functools
import math

import jax
import jax.numpy as jnp
from jax import lax
from jax.experimental import pallas as pl
from jax.experimental.pallas import tpu as pltpu
from jax.sharding import PartitionSpec as P

HEADS = 8
MASKED = -1e30
Y_CHUNKS = 2
BLOCK = 128
LANES = 128
KERNEL_US = 5


def cost(us):
    return pl.CostEstimate(
        flops=int(1000 + us * 1.15e9),
        bytes_accessed=int(1000 + us * 3.69e6),
        transcendentals=int(us * 1e6),
    )
ANY = pl.BlockSpec(memory_space=pl.ANY)
HBM = pl.BlockSpec(memory_space=pltpu.HBM)
VMEM = pl.BlockSpec(memory_space=pltpu.VMEM)


def params(block=0):
    return pltpu.CompilerParams(vmem_limit_bytes=max(24 * 1024 * 1024, 48 * block * block))


def start_copies(pairs, sems):
    copies = [
        pltpu.make_async_copy(source, target, sems.at[at])
        for at, (source, target) in enumerate(pairs)
    ]
    for copy in copies:
        copy.start()
    return copies


def normalize(field, gain):
    scale = lax.rsqrt(jnp.mean(field * field, axis=-1, keepdims=True) + 1e-05)
    return field * scale * gain


def line_bias(block, line_of):
    key_at = lax.broadcasted_iota(jnp.int32, (block, 2 * block), 0)
    query_at = lax.rem(lax.broadcasted_iota(jnp.int32, (block, 2 * block), 1), block)
    return jnp.where(line_of(key_at) == line_of(query_at), 0.0, MASKED).astype(jnp.float32)


def project(normed_ref, w_ref, w_values_ref, qk_ref, values_ref):
    total, width = normed_ref.shape
    step = min(256, total)
    for at in range(0, total, step):
        rows = normed_ref[at : at + step]
        qk_ref[at : at + step] = jnp.dot(
            rows, w_ref[:, : 2 * width], preferred_element_type=jnp.float32
        ).astype(jnp.bfloat16)
        values_ref[:, at : at + step] = lax.dot_general(
            w_values_ref[...], rows, (((1,), (1,)), ((), ())), preferred_element_type=jnp.float32
        ).astype(jnp.bfloat16)


def attend(qk, values, bias):
    block, width = qk.shape[0], qk.shape[1] // 2
    size = width // HEADS
    factor = math.log2(math.e) / math.sqrt(size)
    lane = lax.broadcasted_iota(jnp.int32, (block, 2 * size), 1)
    mixed = []
    for at in range(0, width, 2 * size):
        queries = qk[:, at : at + 2 * size]
        key_part = qk[:, width + at : width + at + 2 * size]
        zero = jnp.zeros_like(queries)
        pair = jnp.concatenate(
            [jnp.where(lane < size, queries, zero), jnp.where(lane < size, zero, queries)], axis=0
        )
        scores = lax.dot_general(
            key_part, pair, (((1,), (1,)), ((), ())), preferred_element_type=jnp.float32
        )
        scores = scores + bias
        expo = jnp.exp2((scores - jnp.max(scores, axis=0, keepdims=True)) * factor)
        inverse = 1.0 / jnp.sum(expo, axis=0, keepdims=True)
        expo = expo.astype(jnp.bfloat16)
        for head in range(2):
            rows = slice(at + head * size, at + (head + 1) * size)
            columns = slice(head * block, (head + 1) * block)
            summed = jnp.dot(values[rows], expo[:, columns], preferred_element_type=jnp.float32)
            mixed.append(summed * inverse[:, columns])
    return jnp.concatenate(mixed, axis=0).T


def attention_kernel(plan, gain_ref, w_ref, w_values_ref, *refs):
    operands, results = refs[: plan["operands"]], refs[plan["first_result"] : plan["scratch"]]
    normed_ref, qk_ref, values_ref, bias_ref, *order_refs = refs[plan["scratch"] :]
    block, count = plan["block"], plan["count"]
    bias_ref[...] = line_bias(block, plan["line_of"])
    for index in range(count):
        plan["norm"](index, operands, gain_ref[...], normed_ref, *order_refs)
    project(normed_ref, w_ref, w_values_ref, qk_ref, values_ref)
    each = normed_ref.shape[0] // count
    for index in range(count):
        for at in range(index * each, (index + 1) * each, block):
            out = attend(qk_ref[at : at + block], values_ref[:, at : at + block], bias_ref[...])
            plan["put"](index, at - index * each, out, results, *order_refs)


def attention(plan, total, out_shapes, operands, gain, w_qkv, w_values, after, name):
    width = w_qkv.shape[0]
    block = plan["block"]
    inputs = [gain, w_qkv, w_values, *operands, *after]
    plan = dict(
        plan,
        operands=len(operands),
        first_result=len(operands) + len(after),
        scratch=len(operands) + len(after) + len(out_shapes),
    )
    bf16, f32 = jnp.bfloat16, jnp.float32
    return pl.pallas_call(
        functools.partial(attention_kernel, plan),
        out_shape=[jax.ShapeDtypeStruct(shape, bf16) for shape in out_shapes],
        in_specs=[VMEM] * (3 + len(operands)) + [ANY] * len(after),
        out_specs=[VMEM] * len(out_shapes),
        scratch_shapes=[
            pltpu.VMEM((total, width), bf16),
            pltpu.VMEM((total, 2 * width), bf16),
            pltpu.VMEM((width, total), bf16),
            pltpu.VMEM((block, 2 * block), f32),
            *[pltpu.VMEM(shape, f32) for shape in plan["order"]],
        ],
        compiler_params=params(block),
        cost_estimate=cost(KERNEL_US),
        name=name,
    )(*inputs)


def attend_time(tokens, gain, w_qkv, w_values, after=()):
    batch, steps, cells_x, cells_y, width = tokens.shape
    block = steps * cells_y
    count = batch * cells_x

    def norm(index, operands, gain, normed):
        field = operands[0][index // cells_x, :, index % cells_x].astype(jnp.float32)
        field = normalize(field.reshape(block, width), gain)
        normed[index * block : (index + 1) * block] = field.astype(jnp.bfloat16)

    def put(index, at, out, results):
        field = out.reshape(steps, cells_y, width).astype(jnp.bfloat16)
        results[0][index // cells_x, :, index % cells_x] = field

    plan = dict(
        block=block,
        count=count,
        line_of=lambda at: lax.rem(at, cells_y),
        norm=norm,
        put=put,
        order=[],
    )
    return attention(
        plan, count * block, [tokens.shape], [tokens], gain, w_qkv, w_values, after, "attend_time"
    )[0]


def attend_y(pieces, first, planes, gain, w_qkv, w_values, after=()):
    size = len(pieces)
    _, cells_x, cells_y, width = pieces[0].shape
    block = size * cells_x * cells_y

    def norm(index, operands, gain, normed):
        field = jnp.concatenate(
            [ref[first + index].astype(jnp.float32).reshape(cells_x * cells_y, width) for ref in operands],
            axis=0,
        )
        normed[index * block : (index + 1) * block] = normalize(field, gain).astype(jnp.bfloat16)

    def put(index, at, out, results):
        field = out.reshape(size, cells_x, cells_y, width).astype(jnp.bfloat16)
        for part in range(size):
            results[part][index] = field[part]

    plan = dict(
        block=block,
        count=planes,
        line_of=lambda at: lax.rem(lax.div(at, cells_y), cells_x),
        norm=norm,
        put=put,
        order=[],
    )
    shapes = [(planes, cells_x, cells_y, width)] * size
    return attention(
        plan, planes * block, shapes, pieces, gain, w_qkv, w_values, after, "attend_y"
    )


def attend_x(pieces, gain, w_qkv, w_values, after=()):
    size, planes, cells_x, cells_y, width = pieces.shape
    chips = size // 2
    length = size * cells_x
    each = length * cells_y
    together = max(1, min(cells_y, BLOCK // length))
    block = together * length
    columns = [slice(at, at + LANES) for at in range(0, width, LANES)]

    def norm(index, operands, gain, normed, order):
        field = operands[0][:, index].astype(jnp.float32).reshape(each, width)
        field = normalize(field, gain)
        for part, lanes in enumerate(columns):
            order[part] = field[:, lanes]
        for y in range(cells_y):
            at = index * each + y * length
            for part, lanes in enumerate(columns):
                line = order[part, pl.ds(y, length, stride=cells_y), :]
                normed[at : at + length, lanes] = line.astype(jnp.bfloat16)

    def put(index, at, out, results, order):
        for line in range(together):
            rows = slice(line * length, (line + 1) * length)
            for part, lanes in enumerate(columns):
                where = pl.ds(at // length + line, length, stride=cells_y)
                order[part, where, :] = out[rows, lanes]
        if at + block < each:
            return
        device = lax.axis_index("gx")
        chip, core = device // 2, lax.rem(device, 2)
        per = cells_x * cells_y
        for flip in range(chips):
            for which, lane in enumerate((core, 1 - core)):
                start = pl.multiple_of(((chip ^ flip) * 2 + lane) * per, per)
                for part, lanes in enumerate(columns):
                    field = order[part, pl.ds(start, per), :].reshape(cells_x, cells_y, LANES)
                    results[flip][which, index, :, :, lanes] = field.astype(jnp.bfloat16)

    plan = dict(
        block=block,
        count=planes,
        line_of=lambda at: lax.div(at, length),
        norm=norm,
        put=put,
        order=[(width // LANES, each, LANES)],
    )
    shapes = [(2, planes, cells_x, cells_y, width)] * chips
    return attention(
        plan, planes * each, shapes, [pieces], gain, w_qkv, w_values, after, "attend_x"
    )


def pack_kernel(count, *refs):
    out, sems = refs[-2:]
    for copy in start_copies([(refs[at].at[1], out.at[at]) for at in range(count)], sems):
        copy.wait()


def pack(pieces):
    count = len(pieces)
    return pl.pallas_call(
        functools.partial(pack_kernel, count),
        out_shape=jax.ShapeDtypeStruct((count,) + pieces[0].shape[1:], pieces[0].dtype),
        in_specs=[VMEM] * count,
        out_specs=VMEM,
        scratch_shapes=[pltpu.SemaphoreType.DMA((count,))],
        compiler_params=params(),
        cost_estimate=cost(0),
        name="pack_x",
    )(*pieces)


def base_kernel(count, along_time_ref, *refs):
    pieces, sibling, out_ref = refs[:count], refs[count], refs[-1]
    planes = pieces[0].shape[1]
    device = lax.axis_index("gx")
    chip, core = device // 2, lax.rem(device, 2)
    for index in range(count):
        for lane, source in ((core, pieces[index].at[0]), (1 - core, sibling.at[index])):
            at = pl.ds(((chip ^ index) * 2 + lane) * planes, planes)
            out_ref[at] = along_time_ref[at].astype(jnp.float32) + source[...].astype(jnp.float32)


def add_x(along_time, pieces, sibling):
    return pl.pallas_call(
        functools.partial(base_kernel, len(pieces)),
        out_shape=jax.ShapeDtypeStruct(along_time.shape, jnp.float32),
        in_specs=[VMEM] * (2 + len(pieces)),
        out_specs=VMEM,
        compiler_params=params(),
        cost_estimate=cost(0),
        name="add_x",
    )(along_time, *pieces, sibling)


def final_kernel(size, flips, first, w_ref, tokens_ref, base_ref, *refs):
    pieces = refs[: len(flips)]
    out_ref, held_ref, sems = refs[-3:]
    _, planes, cells_x, cells_y, width = held_ref.shape
    group = tokens_ref.shape[0] // size
    me = lax.axis_index("gy")
    storing = []
    for at, flip in enumerate(flips):
        where = pl.ds((me ^ flip) * group + first, planes)
        mixed = base_ref[where] + pieces[at][...].astype(jnp.float32)
        mixed = mixed.reshape(planes * cells_x * cells_y, width).astype(jnp.bfloat16)
        update = jnp.dot(mixed, w_ref[...], preferred_element_type=jnp.float32)
        field = tokens_ref[where].astype(jnp.float32)
        held_ref[at] = (field + update.reshape(field.shape)).astype(jnp.bfloat16)
        copy = pltpu.make_async_copy(held_ref.at[at], out_ref.at[where], sems.at[at])
        copy.start()
        storing.append(copy)
    for copy in storing:
        copy.wait()


def finish(size, flips, first, w_out, tokens, base, pieces, result):
    count = len(flips)
    earlier = [] if result is None else [result]
    return pl.pallas_call(
        functools.partial(final_kernel, size, flips, first),
        out_shape=jax.ShapeDtypeStruct(tokens.shape, tokens.dtype),
        in_specs=[VMEM] * (3 + count) + [ANY] * len(earlier),
        out_specs=ANY,
        scratch_shapes=[
            pltpu.VMEM((count,) + pieces[0].shape, tokens.dtype),
            pltpu.SemaphoreType.DMA((count,)),
        ],
        input_output_aliases={3 + count: 0} if earlier else {},
        compiler_params=params(),
        cost_estimate=cost(0),
        name="finish",
    )(w_out, tokens, base, *pieces, *earlier)


def cut_kernel(flips, planes, tokens_ref, *refs):
    outs, sems = refs[:-1], refs[-1]
    me = lax.axis_index("gy")
    pairs = [
        (tokens_ref.at[pl.ds((me ^ flip) * planes, planes)], out) for flip, out in zip(flips, outs)
    ]
    for copy in start_copies(pairs, sems):
        copy.wait()


def cut(tokens, flips, planes):
    size = len(flips)
    piece = jax.ShapeDtypeStruct((planes,) + tokens.shape[1:], tokens.dtype)
    return pl.pallas_call(
        functools.partial(cut_kernel, flips, planes),
        out_shape=[piece] * size,
        in_specs=[ANY],
        out_specs=[HBM] * size,
        scratch_shapes=[pltpu.SemaphoreType.DMA((size,))],
        compiler_params=params(),
        cost_estimate=cost(0),
        name="cut",
    )(tokens)


def trade(pieces, flips, axis="gy", factor=1):
    size = factor * len(pieces)
    return [
        piece
        if flip == 0
        else lax.ppermute(piece, axis, [(at, at ^ (factor * flip)) for at in range(size)])
        for flip, piece in zip(flips, pieces)
    ]


def body(count_x, count_y, tokens, norm_gain, w_qkv, w_out):
    batch, steps, cells_x, cells_y, width = tokens.shape
    lines = batch * steps
    plane_shape = (cells_x, cells_y, width)
    gain = norm_gain.reshape(1, width)
    chunks = math.gcd(Y_CHUNKS, lines // count_y)
    chunk_planes = lines // count_y // chunks
    flat = tokens.reshape((lines,) + plane_shape)
    w_values = w_qkv[:, 2 * width :].T

    swap = [(at, at ^ 1) for at in range(count_x)]
    flips = range(count_y)
    y_pieces = trade(cut(flat, flips, lines // count_y), flips)
    along_time = attend_time(tokens, gain, w_qkv, w_values)
    x_pieces = lax.all_to_all(
        flat.reshape((count_x, lines // count_x) + plane_shape), "gx", 0, 0, tiled=True
    )
    along_x = attend_x(x_pieces, gain, w_qkv, w_values, [along_time])
    last = along_x[0]
    returned = []
    for chunk in range(chunks):
        out = attend_y(
            y_pieces, chunk * chunk_planes, chunk_planes, gain, w_qkv, w_values, [last]
        )
        last = out[0]
        returned.append(dict(zip(flips, trade(out, flips))))
    along_x = trade(along_x, range(count_x // 2), "gx", 2)
    sibling = lax.ppermute(pack(along_x), "gx", swap)
    base = add_x(along_time.reshape((lines,) + plane_shape), along_x, sibling)

    result = None
    for chunk, pieces in enumerate(returned):
        near = [*range(count_y // 2)]
        far = [*range(count_y // 2, count_y)]
        for some in [near, far] if chunk == chunks - 1 else [[0, *range(count_y - 1, 0, -1)]]:
            if some:
                result = finish(
                    count_y,
                    some,
                    chunk * chunk_planes,
                    w_out,
                    flat,
                    base,
                    [pieces[flip] for flip in some],
                    result,
                )
    return result.reshape(tokens.shape)


def solution(mesh):
    placed = (P(None, None, "gx", "gy", None), P(), P(), P())
    return jax.shard_map(
        functools.partial(body, mesh.shape["gx"], mesh.shape["gy"]),
        mesh=mesh,
        in_specs=placed,
        out_specs=P(None, None, "gx", "gy", None),
        check_vma=False,
    )
```
